32 devices in a mesh: layer: 4 (over y, x), feat: 8 (over z, core).
Axes of the slice: x: 2, y: 2, z: 4, core: 2. Of those that a mesh axis runs over, the one named last changes fastest.
Arguments:
- residuals: bfloat16 [256, 4096], P('feat', 'layer'), may hold values from -6 to 6
- errors: bfloat16 [256, 4096], P('feat', 'layer'), may hold values from -0.375 to 0.375
- enc_weight: bfloat16 [4096, 65536], P('layer', 'feat'), may hold values from -0.09375 to 0.09375
- dec_weight: bfloat16 [4096, 65536], P('layer', 'feat'), may hold values from -0.09375 to 0.09375
- enc_bias: float32 [65536], P('feat'), may hold values from -3 to 3
Outputs:
- enc_grad: bfloat16 [4096, 65536], P('layer', 'feat')
- dec_grad: bfloat16 [4096, 65536], P('layer', 'feat')
- bias_grad: float32 [65536], P('feat')
The draws below stay inside these ranges and needn't reach their ends.
All inputs are finite; a program needn't handle non-finite values.
Results may differ from the reference program's by a relative error of at most 0.0055.
Values may be sent and summed in bfloat16 or wider, within the bound.
No kernel may reach another device: no remote copies, remote signals or barrier semaphores. Data moves between devices by JAX's collectives and lax.ppermute only.
A program may use at most 128 MiB of HBM per device.

```python
import jax
import jax.numpy as jnp

FEATS = 65536
TOKENS = 256
STACK = 4096


def steps_of(rng, extent, cuts, least, high):
    def one(dim, blocks):
        heights = jax.random.uniform(jax.random.fold_in(jax.random.fold_in(rng, 6), dim), (blocks,), jnp.float32, least / len(cuts), high / len(cuts))
        return jnp.repeat(jnp.exp(heights), extent[dim] // blocks).reshape((-1,) + (1,) * (len(extent) - dim - 1))

    loudness = one(*cuts[0])
    for cut in cuts[1:]:
        loudness = loudness * one(*cut)
    return loudness


def gaussian(stream_key, shape, spread, reach, split=(), held_as=jnp.bfloat16):
    level = steps_of(stream_key, shape, split, -0.22, 0.18) if split else 1.0
    array = jax.random.normal(stream_key, shape, jnp.float32) * spread * level
    return jnp.minimum(jnp.maximum(array, -reach), reach).astype(held_as)


def setup_inputs(seed: int = 0) -> dict:
    seeds = jax.random.split(jax.random.key(seed), 6)
    return {
        "residuals": gaussian(seeds[0], (TOKENS, STACK), 1.0, 6.0, ((0, 8), (1, 4))),
        "errors": gaussian(seeds[1], (TOKENS, STACK), (TOKENS ** -0.5), 0.375, ((0, 8), (1, 4))),
        "enc_weight": gaussian(seeds[2], (STACK, FEATS), STACK ** -0.5, 0.09375, ((0, 4), (1, 8))),
        "dec_weight": gaussian(seeds[3], (STACK, FEATS), STACK ** -0.5, 0.09375, ((0, 4), (1, 8))),
        "enc_bias": gaussian(seeds[4], (FEATS,), 0.5, 3.0, ((0, 8),), jnp.float32),
    }


def reference(residuals, errors, enc_weight, dec_weight, enc_bias):
    preact = jnp.dot(residuals, enc_weight, preferred_element_type=jnp.float32) + enc_bias
    code_grad = jnp.dot(errors, dec_weight, preferred_element_type=jnp.float32)
    code = (jax.nn.softplus(4.0 * preact) / 4.0).astype(jnp.bfloat16)
    masked = (code_grad * jax.nn.sigmoid(4.0 * preact)).astype(jnp.bfloat16)
    enc_grad = jnp.dot(residuals.T, masked, preferred_element_type=jnp.float32).astype(jnp.bfloat16)
    dec_grad = jnp.dot(errors.T, code, preferred_element_type=jnp.float32).astype(jnp.bfloat16)
    bias_grad = jnp.sum(masked.astype(jnp.float32), axis=0)
    return enc_grad, dec_grad, bias_grad
```

```python
import functools

import jax
import jax.numpy as jnp
from jax import lax
from jax.experimental import pallas as pl
from jax.experimental.pallas import tpu as pltpu
from jax.sharding import PartitionSpec as P

BF16 = jnp.bfloat16
F32 = jnp.float32
VMEM_LIMIT = 48 * 2**20


def params():
    return pltpu.CompilerParams(vmem_limit_bytes=VMEM_LIMIT)


def tree_sum(parts):
    while len(parts) > 1:
        parts = [parts[i] + parts[i + 1] for i in range(0, len(parts), 2)]
    return parts[0]


def divisor(extent, most):
    size = min(extent, most)
    while extent % size:
        size -= 128
    return size


class Plan:
    def __init__(self, layers, peers, rows, stack, feats):
        self.layers, self.peers, self.rows = layers, peers, rows
        self.stack, self.feats = stack, feats
        self.bits = layers.bit_length() - 1
        self.blocks = 1 << max(self.bits - 1, 0)
        order = list(range(self.bits))
        self.orders = (order[::-1], order)
        near = 2
        while near < peers and (near * rows) % (32 * self.blocks):
            near *= 2
        self.near = min(near, peers)

    def keys(self):
        me = lax.axis_index("layer")
        out = []
        for order in self.orders:
            key = 0
            for level, bit in enumerate(order[:-1]):
                key = key + (((me >> bit) & 1) << (self.bits - 2 - level))
            out.append(key)
        return out

    def swap(self, array, bit):
        pairs = [(i, i ^ (1 << bit)) for i in range(self.layers)]
        return lax.ppermute(array, "layer", pairs)

    def peer(self, array, distance):
        pairs = [(i, i ^ distance) for i in range(self.peers)]
        return lax.ppermute(array, "feat", pairs)


def place_rows(plan, raws, store):
    keys = plan.keys()
    tokens = len(raws) * plan.rows
    half = tokens // 2
    block = half // plan.blocks
    step = 16
    for start in range(0, tokens, step):
        stream, within = divmod(start, half)
        index, off = divmod(within, block)
        row = stream * half + (index ^ keys[stream]) * block + off
        row = pl.multiple_of(row, step)
        piece, at = divmod(start, plan.rows)
        for q in range(2):
            store(q, row, raws[piece][q, at : at + step, :])


def partial_kernel(plan, count, *refs):
    raws, (enc_ref, dec_ref), outs, (tokens_ref,) = (
        refs[:count],
        refs[count : count + 2],
        refs[count + 2 : -1],
        refs[-1:],
    )

    @pl.when(pl.program_id(0) == 0)
    def _():
        def store(q, row, values):
            tokens_ref[q, pl.ds(row, 16), :] = values

        place_rows(plan, raws, store)

    rows = outs[0].shape[1]
    for q, weight in enumerate((enc_ref, dec_ref)):
        part = jnp.dot(tokens_ref[q], weight[...], preferred_element_type=F32)
        for i, out in enumerate(outs):
            out[q] = part[i * rows : (i + 1) * rows].astype(BF16)


def partials(plan, raws, enc_weight, dec_weight, first, width):
    tokens = len(raws) * plan.rows
    outs = 4 if plan.blocks > 1 else 2
    block = divisor(width, 512)
    base = first // block
    weight = pl.BlockSpec((plan.stack, block), lambda i: (0, base + i))
    raw = pl.BlockSpec((2, plan.rows, plan.stack), lambda i: (0, 0, 0))
    out = pl.BlockSpec((2, tokens // outs, block), lambda i: (0, 0, i))
    return pl.pallas_call(
        functools.partial(partial_kernel, plan, len(raws)),
        grid=(width // block,),
        in_specs=[raw] * len(raws) + [weight] * 2,
        out_specs=[out] * outs,
        out_shape=[jax.ShapeDtypeStruct((2, tokens // outs, width), BF16)] * outs,
        scratch_shapes=[pltpu.VMEM((2, tokens, plan.stack), BF16)],
        compiler_params=params(),
        name="partials",
    )(*raws, enc_weight, dec_weight)


def add_kernel(pieces, *refs):
    outs = refs[4:]
    for stream in range(2):
        total = refs[2 * stream][...].astype(F32) + refs[2 * stream + 1][...].astype(F32)
        rows = total.shape[1] // pieces
        for i in range(pieces):
            outs[stream * pieces + i][...] = total[:, i * rows : (i + 1) * rows].astype(BF16)


def add(plan, kept, got, pieces):
    _, rows, width = kept[0].shape
    block = divisor(width, 1024)
    whole = pl.BlockSpec((2, rows, block), lambda i: (0, 0, i))
    part = pl.BlockSpec((2, rows // pieces, block), lambda i: (0, 0, i))
    return pl.pallas_call(
        functools.partial(add_kernel, pieces),
        grid=(width // block,),
        in_specs=[whole] * 4,
        out_specs=[part] * (2 * pieces),
        out_shape=[jax.ShapeDtypeStruct((2, rows // pieces, width), BF16)] * (2 * pieces),
        compiler_params=params(),
        name="add",
    )(kept[0], got[0], kept[1], got[1])


def gate_kernel(*refs):
    bias = refs[4][...]
    for stream in range(2):
        mine, other = refs[2 * stream], refs[2 * stream + 1]
        scaled = 4.0 * (mine[0].astype(F32) + other[0].astype(F32) + bias)
        code_grad = mine[1].astype(F32) + other[1].astype(F32)
        small = jnp.exp(-jnp.abs(scaled))
        code = 0.25 * (jnp.maximum(scaled, 0.0) + jnp.log1p(small))
        gate = jnp.where(scaled >= 0.0, 1.0, small) / (1.0 + small)
        refs[5 + stream][0] = code.astype(BF16)
        refs[5 + stream][1] = (code_grad * gate).astype(BF16)


def gate(plan, mine, other, bias, first):
    _, rows, width = mine[0].shape
    block = divisor(width, 1024)
    base = first // block
    whole = pl.BlockSpec((2, rows, block), lambda i: (0, 0, i))
    return pl.pallas_call(
        gate_kernel,
        grid=(width // block,),
        in_specs=[whole] * 4 + [pl.BlockSpec((1, block), lambda i: (0, base + i))],
        out_specs=[whole] * 2,
        out_shape=[jax.ShapeDtypeStruct((2, rows, width), BF16)] * 2,
        compiler_params=params(),
        name="gate",
    )(mine[0], other[0], mine[1], other[1], bias)


def turn_kernel(plan, counts, *refs):
    raws, outs, scratch = refs[: sum(counts)], refs[sum(counts) : -1], refs[-1]
    done = 0
    for group, count in enumerate(counts):
        base = done * plan.rows

        def store(q, row, values):
            scratch[q, pl.ds(pl.multiple_of(base + row, 16), 16), :] = values

        place_rows(plan, raws[done : done + count], store)
        done += count
    for q in range(2):
        outs[q][...] = scratch[q].T


def turned(plan, groups):
    counts = [len(group) for group in groups]
    raws = [raw for group in groups for raw in group]
    tokens = len(raws) * plan.rows
    return pl.pallas_call(
        functools.partial(turn_kernel, plan, counts),
        out_shape=[jax.ShapeDtypeStruct((plan.stack, tokens), BF16)] * 2,
        scratch_shapes=[pltpu.VMEM((2, tokens, plan.stack), BF16)],
        compiler_params=params(),
        name="turned",
    )(*raws)


def grads_kernel(sizes, count, aliased, *refs):
    resid_ref, error_ref = refs[:2]
    parts = refs[2 : 2 + count]
    enc_ref, dec_ref, bias_ref, code_ref, masked_ref = refs[2 + count + aliased :]
    row = 0
    at = 0
    sums = []
    for size in sizes:
        blocks = []
        for part in parts[at : at + size]:
            rows = part.shape[1]
            code_ref[row : row + rows] = part[0]
            masked_ref[row : row + rows] = part[1]
            blocks.append(jnp.sum(part[1].astype(F32), axis=0, keepdims=True))
            row += rows
        at += size
        sums.append(tree_sum(blocks))
    total = sums[0]
    for value in sums[1:]:
        total = total + value
    bias_ref[...] = total
    enc_ref[...] = jnp.dot(resid_ref[...], masked_ref[...], preferred_element_type=F32).astype(BF16)
    dec_ref[...] = jnp.dot(error_ref[...], code_ref[...], preferred_element_type=F32).astype(BF16)


def grads(plan, turned_tokens, holdings, first, width, before):
    tokens = turned_tokens[0].shape[1]
    block = divisor(width, 512)
    base = first // block
    parts, specs, sizes = [], [], []
    for arrays, origin in holdings:
        sizes.append(len(arrays))
        skip = (first - origin) // block
        for array in arrays:
            parts.append(array)
            specs.append(
                pl.BlockSpec((2, array.shape[1], block), lambda i, skip=skip: (0, 0, skip + i))
            )
    whole = pl.BlockSpec((plan.stack, tokens), lambda i: (0, 0))
    aliased = [] if before is None else list(before)
    shapes = [
        jax.ShapeDtypeStruct((plan.stack, plan.feats), BF16),
        jax.ShapeDtypeStruct((plan.stack, plan.feats), BF16),
        jax.ShapeDtypeStruct((1, plan.feats), F32),
    ]
    return pl.pallas_call(
        functools.partial(grads_kernel, sizes, len(parts), len(aliased)),
        grid=(width // block,),
        in_specs=[whole] * 2 + specs + [pl.BlockSpec(memory_space=pl.ANY)] * len(aliased),
        out_specs=[
            pl.BlockSpec((plan.stack, block), lambda i: (0, base + i)),
            pl.BlockSpec((plan.stack, block), lambda i: (0, base + i)),
            pl.BlockSpec((1, block), lambda i: (0, base + i)),
        ],
        out_shape=shapes,
        scratch_shapes=[pltpu.VMEM((tokens, block), BF16)] * 2,
        input_output_aliases={2 + len(parts) + i: i for i in range(len(aliased))},
        compiler_params=params(),
        name="grads",
    )(*turned_tokens, *parts, *aliased)


def reduce_gate_gather(plan, outs, bias, first):
    if plan.blocks > 1:
        kept, sent = [outs[0], outs[2]], [outs[1], outs[3]]
    else:
        kept = list(outs)
    levels = plan.bits - 1
    for level in range(levels):
        got = [plan.swap(sent[s], plan.orders[s][level]) for s in range(2)]
        pieces = 2 if level < levels - 1 else 1
        cut = add(plan, kept, got, pieces)
        if pieces == 2:
            kept, sent = [cut[0], cut[2]], [cut[1], cut[3]]
        else:
            kept = list(cut)
    other = [plan.swap(kept[s], plan.orders[s][-1]) for s in range(2)]
    gated = gate(plan, kept, other, bias, first)
    held = [[gated[0]], [gated[1]]]
    for level in reversed(range(levels)):
        for s in range(2):
            held[s] = held[s] + [plan.swap(a, plan.orders[s][level]) for a in held[s]]
    return held


def per_device(plan, residuals, errors, enc_weight, dec_weight, enc_bias):
    feats = plan.feats
    bias = enc_bias.reshape(1, feats)
    own = jnp.stack([residuals, errors])
    near = [own] + [plan.peer(own, m) for m in range(1, plan.near)]
    far = []
    for m in range(plan.near, plan.peers, 2):
        came = plan.peer(own, m)
        far += [came, plan.peer(came, 1)]
    quarter = feats // 4
    near_cuts = [(0, quarter), (quarter, feats - quarter)]
    far_cuts = [(i * quarter, quarter) for i in range(4)]

    near_held = []
    for first, width in near_cuts:
        outs = partials(plan, near, enc_weight, dec_weight, first, width)
        near_held.append((first, width, reduce_gate_gather(plan, outs, bias, first)))
    flipped = turned(plan, [near, far] if far else [near])
    result = None
    for first, width in far_cuts:
        holdings = []
        for start, extent, held in near_held:
            if start <= first < start + extent:
                holdings += [(held[0], start), (held[1], start)]
        if far:
            outs = partials(plan, far, enc_weight, dec_weight, first, width)
            held = reduce_gate_gather(plan, outs, bias, first)
            holdings += [(held[0], first), (held[1], first)]
        result = grads(plan, flipped, holdings, first, width, result)
    enc_grad, dec_grad, bias_grad = result
    return enc_grad, dec_grad, bias_grad.reshape(feats)


def solution(mesh):
    placed = (
        P("feat", "layer"),
        P("feat", "layer"),
        P("layer", "feat"),
        P("layer", "feat"),
        P("feat"),
    )
    layers, peers = mesh.shape["layer"], mesh.shape["feat"]

    def body(residuals, errors, enc_weight, dec_weight, enc_bias):
        plan = Plan(layers, peers, residuals.shape[0], residuals.shape[1], enc_bias.shape[0])
        return per_device(plan, residuals, errors, enc_weight, dec_weight, enc_bias)

    return jax.shard_map(
        body,
        mesh=mesh,
        in_specs=placed,
        out_specs=(P("layer", "feat"), P("layer", "feat"), P("feat")),
        check_vma=False,
    )
```

```python
import functools
import math

import jax
import jax.numpy as jnp
from jax import lax
from jax.experimental import pallas as pl
from jax.experimental.pallas import tpu as pltpu
from jax.sharding import PartitionSpec as P

BF16 = jnp.bfloat16
F32 = jnp.float32
VMEM_LIMIT = 48 * 2**20


def params():
    return pltpu.CompilerParams(vmem_limit_bytes=VMEM_LIMIT)


def waiting(after):
    return [pl.BlockSpec(memory_space=pl.ANY)] * len(after)


def tree_sum(parts):
    while len(parts) > 1:
        parts = [parts[i] + parts[i + 1] for i in range(0, len(parts), 2)]
    return parts[0]


def divisor(extent, most):
    size = min(extent, most)
    while extent % size:
        size -= 128
    return size


class Plan:
    def __init__(self, layers, peers, rows, stack, feats):
        self.layers, self.peers, self.rows = layers, peers, rows
        self.stack, self.feats = stack, feats
        self.bits = layers.bit_length() - 1
        self.blocks = 1 << max(self.bits - 1, 0)
        order = list(range(self.bits))
        self.orders = (order[::-1], order)
        near = 2
        while near < peers and (near * rows) % (32 * self.blocks):
            near *= 2
        self.near = min(near, peers)

    def block_rows(self, group):
        return group * self.rows // (2 * self.blocks)

    def keys(self):
        me = lax.axis_index("layer")
        out = []
        for order in self.orders:
            key = 0
            for level, bit in enumerate(order[:-1]):
                key = key + (((me >> bit) & 1) << (self.bits - 2 - level))
            out.append(key)
        return out

    def swap(self, array, bit):
        pairs = [(i, i ^ (1 << bit)) for i in range(self.layers)]
        return lax.ppermute(array, "layer", pairs)

    def peer(self, array, distance):
        pairs = [(i, i ^ distance) for i in range(self.peers)]
        return lax.ppermute(array, "feat", pairs)


def place_rows(plan, groups, raws, store):
    keys = plan.keys()
    heights = [plan.block_rows(group) for group in groups]
    step = 16
    first = base = 0
    for group, block in zip(groups, heights):
        for start in range(0, group * plan.rows, step):
            stream, within = divmod(start, block * plan.blocks)
            index, off = divmod(within, block)
            row = (stream * plan.blocks + (index ^ keys[stream])) * sum(heights) + base + off
            row = pl.multiple_of(row, step)
            piece, at = divmod(start, plan.rows)
            for q in range(2):
                store(q, row, raws[first + piece][q, at : at + step, :])
        first += group
        base += block


def partial_kernel(plan, groups, waits, *refs):
    count = sum(groups)
    raws, (enc_ref, dec_ref), outs, (tokens_ref,) = (
        refs[:count],
        refs[count : count + 2],
        refs[count + 2 + waits : -1],
        refs[-1:],
    )

    @pl.when(pl.program_id(0) == 0)
    def _():
        def store(q, row, values):
            tokens_ref[q, pl.ds(row, 16), :] = values

        place_rows(plan, groups, raws, store)

    rows = outs[0].shape[1]
    for q, weight in enumerate((enc_ref, dec_ref)):
        part = jnp.dot(tokens_ref[q], weight[...], preferred_element_type=F32)
        for i, out in enumerate(outs):
            out[q] = part[i * rows : (i + 1) * rows].astype(BF16)


def partials(plan, groups, raws, enc_weight, dec_weight, first, width, after):
    tokens = len(raws) * plan.rows
    outs = 4 if plan.blocks > 1 else 2
    block = divisor(math.gcd(first, width), 1024)
    base = first // block
    weight = pl.BlockSpec((plan.stack, block), lambda i: (0, base + i))
    raw = pl.BlockSpec((2, plan.rows, plan.stack), lambda i: (0, 0, 0))
    out = pl.BlockSpec((2, tokens // outs, block), lambda i: (0, 0, i))
    return pl.pallas_call(
        functools.partial(partial_kernel, plan, groups, len(after)),
        grid=(width // block,),
        in_specs=[raw] * len(raws) + [weight] * 2 + waiting(after),
        out_specs=[out] * outs,
        out_shape=[jax.ShapeDtypeStruct((2, tokens // outs, width), BF16)] * outs,
        scratch_shapes=[pltpu.VMEM((2, tokens, plan.stack), BF16)],
        compiler_params=params(),
        name="partials",
    )(*raws, enc_weight, dec_weight, *after)


def add_kernel(pieces, waits, *refs):
    outs = refs[4 + waits :]
    for stream in range(2):
        total = refs[2 * stream][...].astype(F32) + refs[2 * stream + 1][...].astype(F32)
        rows = total.shape[1] // pieces
        for i in range(pieces):
            outs[stream * pieces + i][...] = total[:, i * rows : (i + 1) * rows].astype(BF16)


def add(plan, kept, got, pieces, after):
    _, rows, width = kept[0].shape
    block = divisor(width, 1024)
    whole = pl.BlockSpec((2, rows, block), lambda i: (0, 0, i))
    part = pl.BlockSpec((2, rows // pieces, block), lambda i: (0, 0, i))
    return pl.pallas_call(
        functools.partial(add_kernel, pieces, len(after)),
        grid=(width // block,),
        in_specs=[whole] * 4 + waiting(after),
        out_specs=[part] * (2 * pieces),
        out_shape=[jax.ShapeDtypeStruct((2, rows // pieces, width), BF16)] * (2 * pieces),
        compiler_params=params(),
        name="add",
    )(kept[0], got[0], kept[1], got[1], *after)


def gate_kernel(waits, *refs):
    outs = refs[5 + waits :]
    bias = refs[4][...]
    for stream in range(2):
        mine, other = refs[2 * stream], refs[2 * stream + 1]
        scaled = 4.0 * (mine[0].astype(F32) + other[0].astype(F32) + bias)
        code_grad = mine[1].astype(F32) + other[1].astype(F32)
        small = jnp.exp(-jnp.abs(scaled))
        code = 0.25 * (jnp.maximum(scaled, 0.0) + jnp.log1p(small))
        gate = jnp.where(scaled >= 0.0, 1.0, small) / (1.0 + small)
        outs[stream][0] = code.astype(BF16)
        outs[stream][1] = (code_grad * gate).astype(BF16)


def gate(plan, mine, other, bias, first, after):
    _, rows, width = mine[0].shape
    block = divisor(math.gcd(first, width), 1024)
    base = first // block
    whole = pl.BlockSpec((2, rows, block), lambda i: (0, 0, i))
    return pl.pallas_call(
        functools.partial(gate_kernel, len(after)),
        grid=(width // block,),
        in_specs=[whole] * 4 + [pl.BlockSpec((1, block), lambda i: (0, base + i))] + waiting(after),
        out_specs=[whole] * 2,
        out_shape=[jax.ShapeDtypeStruct((2, rows, width), BF16)] * 2,
        compiler_params=params(),
        name="gate",
    )(mine[0], other[0], mine[1], other[1], bias, *after)


def turn_kernel(plan, groups, waits, *refs):
    raws, outs, scratch = refs[: sum(groups)], refs[sum(groups) + waits : -1], refs[-1]

    def store(q, row, values):
        scratch[q, pl.ds(row, 16), :] = values

    place_rows(plan, groups, raws, store)
    for q in range(2):
        outs[q][...] = scratch[q].T


def turned(plan, groups, raws, after):
    tokens = len(raws) * plan.rows
    whole = pl.BlockSpec(memory_space=pltpu.VMEM)
    return pl.pallas_call(
        functools.partial(turn_kernel, plan, groups, len(after)),
        in_specs=[whole] * len(raws) + waiting(after),
        out_specs=[whole] * 2,
        out_shape=[jax.ShapeDtypeStruct((plan.stack, tokens), BF16)] * 2,
        scratch_shapes=[pltpu.VMEM((2, tokens, plan.stack), BF16)],
        compiler_params=params(),
        name="turned",
    )(*raws, *after)


def grads_kernel(rows, skips, waits, *refs):
    resid_ref, error_ref = refs[:2]
    parts = refs[2 : 2 + len(skips)]
    enc_ref, dec_ref, bias_ref, code_ref, masked_ref = refs[2 + len(skips) + waits :]
    block = code_ref.shape[1]
    here = pl.program_id(0) * block
    left = iter(zip(parts, skips))
    total = None
    for stream in rows:
        blocks = []
        for row in stream:
            part, skip = next(left)
            height = part.shape[1]
            columns = pl.ds(pl.multiple_of(skip + here, 128), block)
            masked = part[1, :, columns]
            code_ref[row : row + height] = part[0, :, columns]
            masked_ref[row : row + height] = masked
            blocks.append(jnp.sum(masked.astype(F32), axis=0, keepdims=True))
        value = tree_sum(blocks)
        total = value if total is None else total + value
    bias_ref[...] = total
    enc_ref[...] = jnp.dot(resid_ref[...], masked_ref[...], preferred_element_type=F32).astype(BF16)
    dec_ref[...] = jnp.dot(error_ref[...], code_ref[...], preferred_element_type=F32).astype(BF16)


def grads(plan, turned_tokens, held, first, width, before, after):
    tokens = turned_tokens[0].shape[1]
    block = divisor(math.gcd(first, width), 1024)
    base = first // block
    parts, skips = [], []
    for arrays, _, origin in held:
        parts += arrays
        skips += [first - origin] * len(arrays)
    inside = pl.BlockSpec(memory_space=pltpu.VMEM)
    extra = list(before) + after
    return pl.pallas_call(
        functools.partial(grads_kernel, [rows for _, rows, _ in held], skips, len(extra)),
        grid=(width // block,),
        in_specs=[inside] * (2 + len(parts)) + waiting(extra),
        out_specs=[
            pl.BlockSpec((plan.stack, block), lambda i: (0, base + i)),
            pl.BlockSpec((plan.stack, block), lambda i: (0, base + i)),
            pl.BlockSpec((1, block), lambda i: (0, base + i)),
        ],
        out_shape=[
            jax.ShapeDtypeStruct((plan.stack, plan.feats), BF16),
            jax.ShapeDtypeStruct((plan.stack, plan.feats), BF16),
            jax.ShapeDtypeStruct((1, plan.feats), F32),
        ],
        scratch_shapes=[pltpu.VMEM((tokens, block), BF16)] * 2,
        input_output_aliases={2 + len(parts) + i: i for i in range(len(before))},
        compiler_params=params(),
        name="grads",
    )(*turned_tokens, *parts, *extra)


class Piece:
    def __init__(self, plan, which, first, width):
        self.plan, self.first, self.width = plan, first, width
        near, far = plan.near, plan.peers - plan.near
        heights = [plan.block_rows(near), plan.block_rows(far)]
        self.groups = {"near": [near], "far": [far], "all": [near, far]}[which]
        self.skip = plan.near if which == "far" else 0
        base = heights[0] if which == "far" else 0
        self.rows = [
            [(s * plan.blocks + j) * sum(heights) + base for j in range(plan.blocks)]
            for s in range(2)
        ]

    def start(self, raws, enc_weight, dec_weight, after):
        plan = self.plan
        raws = raws[self.skip : self.skip + sum(self.groups)]
        outs = partials(plan, self.groups, raws, enc_weight, dec_weight, self.first, self.width, after)
        self.level = 0
        if plan.blocks > 1:
            self.kept = [outs[0], outs[2]]
            self.swap([outs[1], outs[3]])
        else:
            self.kept = list(outs)
            self.swap(self.kept)
        return outs[0]

    def swap(self, sent):
        self.got = [self.plan.swap(sent[s], self.plan.orders[s][self.level]) for s in range(2)]
        self.level += 1

    def add(self, after):
        last = self.plan.bits - 1
        while self.level <= last:
            pieces = 2 if self.level < last else 1
            cut = add(self.plan, self.kept, self.got, pieces, after)
            after = [cut[0]]
            if pieces == 2:
                self.kept = [cut[0], cut[2]]
                self.swap([cut[1], cut[3]])
            else:
                self.kept = list(cut)
                self.swap(self.kept)
        return after[0]

    def gate(self, bias, after):
        plan = self.plan
        gated = gate(plan, self.kept, self.got, bias, self.first, after)
        self.held = [[gated[0]], [gated[1]]]
        for level in reversed(range(plan.bits - 1)):
            for s in range(2):
                self.held[s] = self.held[s] + [
                    plan.swap(array, plan.orders[s][level]) for array in self.held[s]
                ]
        return gated[0]


PIECES = (("all", 0, 3), ("all", 3, 3), ("all", 6, 3), ("all", 9, 3), ("all", 12, 2), ("all", 14, 2))
GRADS = tuple((first, width) for _, first, width in PIECES)
ORDER = (
    "P0", "P1", "T0", "A0", "A1", "N0", "N1", "P2",
    "G0", "P3", "G1", "A2", "A3", "N2", "N3", "P4",
    "G2", "P5", "G3", "A4", "A5", "N4", "N5", "G4",
    "G5",
)
CHAIN = True


def per_device(plan, residuals, errors, enc_weight, dec_weight, enc_bias):
    feats = plan.feats
    unit = feats // 16
    bias = enc_bias.reshape(1, feats)
    own = jnp.stack([residuals, errors])
    raws = [own] + [plan.peer(own, m) for m in range(1, plan.near)]
    for m in range(plan.near, plan.peers, 2):
        came = plan.peer(own, m)
        raws += [came, plan.peer(came, 1)]

    pieces = [Piece(plan, which, first * unit, width * unit) for which, first, width in PIECES]
    result, tokens, chain = [], {}, []
    for entry in ORDER:
        op, *behind = entry.split("<")
        step, index = op[0], int(op[1:])
        after = list(chain)
        for name in behind:
            if name[0] == "H":
                after += [part[-1] for part in pieces[int(name[1:])].held]
            else:
                after.append(tokens[name])
        if step == "P":
            token = pieces[index].start(raws, enc_weight, dec_weight, after)
        elif step == "A":
            token = pieces[index].add(after)
        elif step == "N":
            token = pieces[index].gate(bias, after)
        elif step == "T":
            flipped = turned(plan, [plan.near, plan.peers - plan.near], raws, after)
            token = flipped[0]
        else:
            first, width = (unit * v for v in GRADS[index])
            held = []
            for piece in pieces:
                if piece.first <= first < piece.first + piece.width:
                    held += [(piece.held[s], piece.rows[s], piece.first) for s in range(2)]
            result = grads(plan, flipped, held, first, width, result, after)
            token = result[2]
        tokens[op] = token
        chain = [token] if CHAIN else []
    enc_grad, dec_grad, bias_grad = result
    return enc_grad, dec_grad, bias_grad.reshape(feats)


def solution(mesh):
    placed = (
        P("feat", "layer"),
        P("feat", "layer"),
        P("layer", "feat"),
        P("layer", "feat"),
        P("feat"),
    )
    layers, peers = mesh.shape["layer"], mesh.shape["feat"]

    def body(residuals, errors, enc_weight, dec_weight, enc_bias):
        plan = Plan(layers, peers, residuals.shape[0], residuals.shape[1], enc_bias.shape[0])
        return per_device(plan, residuals, errors, enc_weight, dec_weight, enc_bias)

    return jax.shard_map(
        body,
        mesh=mesh,
        in_specs=placed,
        out_specs=(P("layer", "feat"), P("layer", "feat"), P("feat")),
        check_vma=False,
    )
```

```python
import functools
import math

import jax
import jax.numpy as jnp
from jax import lax
from jax.experimental import pallas as pl
from jax.experimental.pallas import tpu as pltpu
from jax.sharding import PartitionSpec as P

BF16 = jnp.bfloat16
F32 = jnp.float32
VMEM_LIMIT = 48 * 2**20


def params():
    return pltpu.CompilerParams(vmem_limit_bytes=VMEM_LIMIT)


def waiting(after):
    return [pl.BlockSpec(memory_space=pl.ANY)] * len(after)


def tree_sum(parts):
    while len(parts) > 1:
        parts = [parts[i] + parts[i + 1] for i in range(0, len(parts), 2)]
    return parts[0]


def divisor(extent, most):
    size = min(extent, most)
    while extent % size:
        size -= 128
    return size


class Plan:
    def __init__(self, layers, peers, rows, stack, feats):
        self.layers, self.peers, self.rows = layers, peers, rows
        self.stack, self.feats = stack, feats
        self.bits = layers.bit_length() - 1
        self.blocks = 1 << max(self.bits - 1, 0)
        order = list(range(self.bits))
        self.orders = (order[::-1], order)
        near = 2
        while near < peers and (near * rows) % (32 * self.blocks):
            near *= 2
        self.near = min(near, peers)

    def block_rows(self, group):
        return group * self.rows // (2 * self.blocks)

    def keys(self):
        me = lax.axis_index("layer")
        out = []
        for order in self.orders:
            key = 0
            for level, bit in enumerate(order[:-1]):
                key = key + (((me >> bit) & 1) << (self.bits - 2 - level))
            out.append(key)
        return out

    def swap(self, array, bit):
        pairs = [(i, i ^ (1 << bit)) for i in range(self.layers)]
        return lax.ppermute(array, "layer", pairs)

    def peer(self, array, distance):
        pairs = [(i, i ^ distance) for i in range(self.peers)]
        return lax.ppermute(array, "feat", pairs)


def place_rows(plan, groups, raws, store):
    keys = plan.keys()
    heights = [plan.block_rows(group) for group in groups]
    step = 16
    slabs = iter([(raw, at) for raw in raws for at in range(0, raw.shape[1], step)])
    base = 0
    for group, block in zip(groups, heights):
        for start in range(0, group * plan.rows, step):
            stream, within = divmod(start, block * plan.blocks)
            index, off = divmod(within, block)
            row = (stream * plan.blocks + (index ^ keys[stream])) * sum(heights) + base + off
            row = pl.multiple_of(row, step)
            raw, at = next(slabs)
            for q in range(2):
                store(q, row, raw[q, at : at + step, :])
        base += block


def collect_kernel(waits, *refs):
    out = refs[-1]
    row = 0
    for ref in refs[: -1 - waits]:
        out[:, row : row + ref.shape[1]] = ref[...]
        row += ref.shape[1]


def collect(pieces, after):
    rows = sum(piece.shape[1] for piece in pieces)
    inside = pl.BlockSpec(memory_space=pltpu.VMEM)
    return pl.pallas_call(
        functools.partial(collect_kernel, len(after)),
        in_specs=[inside] * len(pieces) + waiting(after),
        out_specs=inside,
        out_shape=jax.ShapeDtypeStruct((2, rows, pieces[0].shape[2]), BF16),
        compiler_params=params(),
        name="collect",
    )(*pieces, *after)


def partial_kernel(plan, groups, count, waits, *refs):
    raws, (enc_ref, dec_ref), outs, (tokens_ref,) = (
        refs[:count],
        refs[count : count + 2],
        refs[count + 2 + waits : -1],
        refs[-1:],
    )

    @pl.when(pl.program_id(0) == 0)
    def _():
        def store(q, row, values):
            tokens_ref[q, pl.ds(row, 16), :] = values

        place_rows(plan, groups, raws, store)

    rows = outs[0].shape[1]
    for q, weight in enumerate((enc_ref, dec_ref)):
        part = jnp.dot(tokens_ref[q], weight[...], preferred_element_type=F32)
        for i, out in enumerate(outs):
            out[q] = part[i * rows : (i + 1) * rows].astype(BF16)


def partials(plan, groups, raws, enc_weight, dec_weight, first, width, after):
    tokens = sum(groups) * plan.rows
    outs = 4 if plan.blocks > 1 else 2
    block = divisor(math.gcd(first, width), 1024)
    base = first // block
    weight = pl.BlockSpec((plan.stack, block), lambda i: (0, base + i))
    inputs = [pl.BlockSpec(raw.shape, lambda i: (0, 0, 0)) for raw in raws]
    out = pl.BlockSpec((2, tokens // outs, block), lambda i: (0, 0, i))
    return pl.pallas_call(
        functools.partial(partial_kernel, plan, groups, len(raws), len(after)),
        grid=(width // block,),
        in_specs=inputs + [weight] * 2 + waiting(after),
        out_specs=[out] * outs,
        out_shape=[jax.ShapeDtypeStruct((2, tokens // outs, width), BF16)] * outs,
        scratch_shapes=[pltpu.VMEM((2, tokens, plan.stack), BF16)],
        compiler_params=params(),
        name="partials",
    )(*raws, enc_weight, dec_weight, *after)


def joined_kernel(waits, *refs):
    outs = refs[8 + waits :]
    pieces = len(outs) // 2
    for stream in range(2):
        base = 0
        for kept, got in (refs[4 * stream : 4 * stream + 2], refs[4 * stream + 2 : 4 * stream + 4]):
            total = kept[...].astype(F32) + got[...].astype(F32)
            rows = total.shape[1] // pieces
            for i in range(pieces):
                part = total[:, i * rows : (i + 1) * rows]
                outs[stream * pieces + i][:, base : base + rows] = part.astype(BF16)
            base += rows


def joined(plan, near, far, skip, after):
    pieces = plan.blocks // 2
    width = far[0][0].shape[2]
    block = divisor(math.gcd(skip, width), 1024)
    base = skip // block
    operands, specs = [], []
    for stream in range(2):
        for pair, start in ((near[stream], base), (far[stream], 0)):
            for array in pair:
                operands.append(array)
                specs.append(
                    pl.BlockSpec(
                        (2, array.shape[1], block), lambda i, start=start: (0, 0, start + i)
                    )
                )
    rows = (near[0][0].shape[1] + far[0][0].shape[1]) // pieces
    return pl.pallas_call(
        functools.partial(joined_kernel, len(after)),
        grid=(width // block,),
        in_specs=specs + waiting(after),
        out_specs=[pl.BlockSpec((2, rows, block), lambda i: (0, 0, i))] * (2 * pieces),
        out_shape=[jax.ShapeDtypeStruct((2, rows, width), BF16)] * (2 * pieces),
        compiler_params=params(),
        name="joined",
    )(*operands, *after)


def add_kernel(pieces, waits, *refs):
    outs = refs[4 + waits :]
    for stream in range(2):
        total = refs[2 * stream][...].astype(F32) + refs[2 * stream + 1][...].astype(F32)
        rows = total.shape[1] // pieces
        for i in range(pieces):
            outs[stream * pieces + i][...] = total[:, i * rows : (i + 1) * rows].astype(BF16)


def add(plan, kept, got, pieces, after):
    _, rows, width = kept[0].shape
    block = divisor(width, 1024)
    whole = pl.BlockSpec((2, rows, block), lambda i: (0, 0, i))
    part = pl.BlockSpec((2, rows // pieces, block), lambda i: (0, 0, i))
    return pl.pallas_call(
        functools.partial(add_kernel, pieces, len(after)),
        grid=(width // block,),
        in_specs=[whole] * 4 + waiting(after),
        out_specs=[part] * (2 * pieces),
        out_shape=[jax.ShapeDtypeStruct((2, rows // pieces, width), BF16)] * (2 * pieces),
        compiler_params=params(),
        name="add",
    )(kept[0], got[0], kept[1], got[1], *after)


def gate_kernel(waits, *refs):
    outs = refs[5 + waits :]
    bias = refs[4][...]
    for stream in range(2):
        mine, other = refs[2 * stream], refs[2 * stream + 1]
        scaled = 4.0 * (mine[0].astype(F32) + other[0].astype(F32) + bias)
        code_grad = mine[1].astype(F32) + other[1].astype(F32)
        small = jnp.exp(-jnp.abs(scaled))
        code = 0.25 * (jnp.maximum(scaled, 0.0) + jnp.log1p(small))
        gate = jnp.where(scaled >= 0.0, 1.0, small) / (1.0 + small)
        outs[stream][0] = code.astype(BF16)
        outs[stream][1] = (code_grad * gate).astype(BF16)


def gate(plan, mine, other, bias, first, after):
    _, rows, width = mine[0].shape
    block = divisor(math.gcd(first, width), 1024)
    base = first // block
    whole = pl.BlockSpec((2, rows, block), lambda i: (0, 0, i))
    return pl.pallas_call(
        functools.partial(gate_kernel, len(after)),
        grid=(width // block,),
        in_specs=[whole] * 4 + [pl.BlockSpec((1, block), lambda i: (0, base + i))] + waiting(after),
        out_specs=[whole] * 2,
        out_shape=[jax.ShapeDtypeStruct((2, rows, width), BF16)] * 2,
        compiler_params=params(),
        name="gate",
    )(mine[0], other[0], mine[1], other[1], bias, *after)


def turn_kernel(plan, groups, count, waits, *refs):
    raws, outs, scratch = refs[:count], refs[count + waits : -1], refs[-1]

    def store(q, row, values):
        scratch[q, pl.ds(row, 16), :] = values

    place_rows(plan, groups, raws, store)
    for q in range(2):
        outs[q][...] = scratch[q].T


def turned(plan, groups, raws, after):
    tokens = sum(groups) * plan.rows
    whole = pl.BlockSpec(memory_space=pltpu.VMEM)
    return pl.pallas_call(
        functools.partial(turn_kernel, plan, groups, len(raws), len(after)),
        in_specs=[whole] * len(raws) + waiting(after),
        out_specs=[whole] * 2,
        out_shape=[jax.ShapeDtypeStruct((plan.stack, tokens), BF16)] * 2,
        scratch_shapes=[pltpu.VMEM((2, tokens, plan.stack), BF16)],
        compiler_params=params(),
        name="turned",
    )(*raws, *after)


def grads_kernel(rows, skips, waits, *refs):
    resid_ref, error_ref = refs[:2]
    parts = refs[2 : 2 + len(skips)]
    enc_ref, dec_ref, bias_ref, code_ref, masked_ref = refs[2 + len(skips) + waits :]
    block = code_ref.shape[1]
    here = pl.program_id(0) * block
    left = iter(zip(parts, skips))
    total = None
    for stream in rows:
        blocks = []
        for row in stream:
            part, skip = next(left)
            height = part.shape[1]
            columns = pl.ds(pl.multiple_of(skip + here, 128), block)
            masked = part[1, :, columns]
            code_ref[row : row + height] = part[0, :, columns]
            masked_ref[row : row + height] = masked
            blocks.append(jnp.sum(masked.astype(F32), axis=0, keepdims=True))
        value = tree_sum(blocks)
        total = value if total is None else total + value
    bias_ref[...] = total
    enc_ref[...] = jnp.dot(resid_ref[...], masked_ref[...], preferred_element_type=F32).astype(BF16)
    dec_ref[...] = jnp.dot(error_ref[...], code_ref[...], preferred_element_type=F32).astype(BF16)


def grads(plan, turned_tokens, held, first, width, before, after):
    tokens = turned_tokens[0].shape[1]
    block = divisor(math.gcd(first, width), 1024)
    base = first // block
    parts, skips = [], []
    for arrays, _, origin in held:
        parts += arrays
        skips += [first - origin] * len(arrays)
    inside = pl.BlockSpec(memory_space=pltpu.VMEM)
    extra = list(before) + after
    return pl.pallas_call(
        functools.partial(grads_kernel, [rows for _, rows, _ in held], skips, len(extra)),
        grid=(width // block,),
        in_specs=[inside] * (2 + len(parts)) + waiting(extra),
        out_specs=[
            pl.BlockSpec((plan.stack, block), lambda i: (0, base + i)),
            pl.BlockSpec((plan.stack, block), lambda i: (0, base + i)),
            pl.BlockSpec((1, block), lambda i: (0, base + i)),
        ],
        out_shape=[
            jax.ShapeDtypeStruct((plan.stack, plan.feats), BF16),
            jax.ShapeDtypeStruct((plan.stack, plan.feats), BF16),
            jax.ShapeDtypeStruct((1, plan.feats), F32),
        ],
        scratch_shapes=[pltpu.VMEM((tokens, block), BF16)] * 2,
        input_output_aliases={2 + len(parts) + i: i for i in range(len(before))},
        compiler_params=params(),
        name="grads",
    )(*turned_tokens, *parts, *extra)


class Piece:
    def __init__(self, plan, which, first, width):
        self.plan, self.first, self.width = plan, first, width
        near, far = plan.near, plan.peers - plan.near
        heights = [plan.block_rows(near), plan.block_rows(far)]
        self.groups = {"near": [near], "far": [far], "all": [near, far]}[which]
        base = heights[0] if which == "far" else 0
        self.rows = [
            [(s * plan.blocks + j) * sum(heights) + base for j in range(plan.blocks)]
            for s in range(2)
        ]

    def start(self, raws, enc_weight, dec_weight, early, after):
        plan = self.plan
        self.early = early
        groups = self.groups
        if early is not None:
            groups, raws = groups[1:], raws[plan.near :]
        outs = partials(plan, groups, raws, enc_weight, dec_weight, self.first, self.width, after)
        self.level = 0
        if plan.blocks > 1:
            self.kept = [outs[0], outs[2]]
            self.swap([outs[1], outs[3]])
        else:
            self.kept = list(outs)
            self.swap(self.kept)
        return outs[0]

    def swap(self, sent):
        self.got = [self.plan.swap(sent[s], self.plan.orders[s][self.level]) for s in range(2)]
        self.level += 1

    def add(self, after):
        last = self.plan.bits - 1
        while self.level <= last:
            pieces = 2 if self.level < last else 1
            if self.level == 1 and self.early is not None:
                near = list(zip(self.early.kept, self.early.got))
                far = list(zip(self.kept, self.got))
                cut = joined(self.plan, near, far, self.first - self.early.first, after)
            else:
                cut = add(self.plan, self.kept, self.got, pieces, after)
            after = [cut[0]]
            if pieces == 2:
                self.kept = [cut[0], cut[2]]
                self.swap([cut[1], cut[3]])
            else:
                self.kept = list(cut)
                self.swap(self.kept)
        return after[0]

    def gate(self, bias, after):
        plan = self.plan
        gated = gate(plan, self.kept, self.got, bias, self.first, after)
        self.held = [[gated[0]], [gated[1]]]
        for level in reversed(range(plan.bits - 1)):
            for s in range(2):
                self.held[s] = self.held[s] + [
                    plan.swap(array, plan.orders[s][level]) for array in self.held[s]
                ]
        return gated[0]


PIECES = (("all", 0, 3), ("all", 3, 3), ("all", 6, 3), ("all", 9, 3), ("all", 12, 2), ("all", 14, 2))
GRADS = tuple((first, width) for _, first, width in PIECES)
ORDER = (
    "P0", "P1", "T0", "A0", "A1", "N0", "N1", "P2",
    "G0", "P3", "G1", "A2", "A3", "N2", "N3", "P4",
    "G2", "P5", "G3", "A4", "A5", "N4", "N5", "G4",
    "G5",
)
CHAIN = True
AHEAD = 2


def per_device(plan, residuals, errors, enc_weight, dec_weight, enc_bias):
    feats = plan.feats
    unit = feats // 16
    bias = enc_bias.reshape(1, feats)
    own = jnp.stack([residuals, errors])
    raws = [own] + [plan.peer(own, m) for m in range(1, plan.near)]
    far = [plan.peer(own, m) for m in range(plan.near, plan.peers, 2)]

    pieces = [Piece(plan, which, first * unit, width * unit) for which, first, width in PIECES]
    result, tokens, chain = [], {}, []
    early = None
    if AHEAD and plan.bits > 1 and plan.near < plan.peers:
        ahead = pieces[:AHEAD]
        width = sum(piece.width for piece in ahead)
        early = Piece(plan, "near", ahead[0].first, width)
        chain = [early.start(raws, enc_weight, dec_weight, None, [])]
    if far:
        mine = collect(far, chain)
        raws += [mine, plan.peer(mine, 1)]
    for entry in ORDER:
        op, *behind = entry.split("<")
        step, index = op[0], int(op[1:])
        after = list(chain)
        for name in behind:
            if name[0] == "H":
                after += [part[-1] for part in pieces[int(name[1:])].held]
            else:
                after.append(tokens[name])
        if step == "P":
            covers = early is not None and index < AHEAD
            if covers and index == AHEAD - 1:
                after = after + early.got
            token = pieces[index].start(
                raws, enc_weight, dec_weight, early if covers else None, after
            )
        elif step == "A":
            token = pieces[index].add(after)
        elif step == "N":
            token = pieces[index].gate(bias, after)
        elif step == "T":
            flipped = turned(plan, [plan.near, plan.peers - plan.near], raws, after)
            token = flipped[0]
        else:
            first, width = (unit * v for v in GRADS[index])
            held = []
            for piece in pieces:
                if piece.first <= first < piece.first + piece.width:
                    held += [(piece.held[s], piece.rows[s], piece.first) for s in range(2)]
            result = grads(plan, flipped, held, first, width, result, after)
            token = result[2]
        tokens[op] = token
        chain = [token] if CHAIN else []
    enc_grad, dec_grad, bias_grad = result
    return enc_grad, dec_grad, bias_grad.reshape(feats)


def solution(mesh):
    placed = (
        P("feat", "layer"),
        P("feat", "layer"),
        P("layer", "feat"),
        P("layer", "feat"),
        P("feat"),
    )
    layers, peers = mesh.shape["layer"], mesh.shape["feat"]

    def body(residuals, errors, enc_weight, dec_weight, enc_bias):
        plan = Plan(layers, peers, residuals.shape[0], residuals.shape[1], enc_bias.shape[0])
        return per_device(plan, residuals, errors, enc_weight, dec_weight, enc_bias)

    return jax.shard_map(
        body,
        mesh=mesh,
        in_specs=placed,
        out_specs=(P("layer", "feat"), P("layer", "feat"), P("feat")),
        check_vma=False,
    )
```

```python
import functools
import math

import jax
import jax.numpy as jnp
from jax import lax
from jax.experimental import pallas as pl
from jax.experimental.pallas import tpu as pltpu
from jax.sharding import PartitionSpec as P

BF16 = jnp.bfloat16
F32 = jnp.float32
VMEM_LIMIT = 48 * 2**20


def params():
    return pltpu.CompilerParams(vmem_limit_bytes=VMEM_LIMIT)


def waiting(after):
    return [pl.BlockSpec(memory_space=pl.ANY)] * len(after)


def tree_sum(parts):
    while len(parts) > 1:
        parts = [parts[i] + parts[i + 1] for i in range(0, len(parts), 2)]
    return parts[0]


def divisor(extent, most):
    size = min(extent, most)
    while extent % size:
        size -= 128
    return size


class Plan:
    def __init__(self, layers, peers, rows, stack, feats):
        self.layers, self.peers, self.rows = layers, peers, rows
        self.stack, self.feats = stack, feats
        self.bits = layers.bit_length() - 1
        self.blocks = 1 << max(self.bits - 1, 0)
        order = list(range(self.bits))
        self.orders = (order[::-1], order)
        near = 2
        while near < peers and (near * rows) % (32 * self.blocks):
            near *= 2
        self.near = min(near, peers)

    def block_rows(self, group):
        return group * self.rows // (2 * self.blocks)

    def keys(self):
        me = lax.axis_index("layer")
        out = []
        for order in self.orders:
            key = 0
            for level, bit in enumerate(order[:-1]):
                key = key + (((me >> bit) & 1) << (self.bits - 2 - level))
            out.append(key)
        return out

    def swap(self, array, bit):
        pairs = [(i, i ^ (1 << bit)) for i in range(self.layers)]
        return lax.ppermute(array, "layer", pairs)

    def peer(self, array, distance):
        pairs = [(i, i ^ distance) for i in range(self.peers)]
        return lax.ppermute(array, "feat", pairs)


def place_rows(plan, groups, raws, store):
    keys = plan.keys()
    heights = [plan.block_rows(group) for group in groups]
    step = 16
    slabs = iter([(raw, at) for raw in raws for at in range(0, raw.shape[1], step)])
    base = 0
    for group, block in zip(groups, heights):
        for start in range(0, group * plan.rows, step):
            stream, within = divmod(start, block * plan.blocks)
            index, off = divmod(within, block)
            row = (stream * plan.blocks + (index ^ keys[stream])) * sum(heights) + base + off
            row = pl.multiple_of(row, step)
            raw, at = next(slabs)
            for q in range(2):
                store(q, row, raw[q, at : at + step, :])
        base += block


def collect_kernel(waits, *refs):
    out = refs[-1]
    row = 0
    for ref in refs[: -1 - waits]:
        out[:, row : row + ref.shape[1]] = ref[...]
        row += ref.shape[1]


def collect(pieces, after):
    rows = sum(piece.shape[1] for piece in pieces)
    inside = pl.BlockSpec(memory_space=pltpu.VMEM)
    return pl.pallas_call(
        functools.partial(collect_kernel, len(after)),
        in_specs=[inside] * len(pieces) + waiting(after),
        out_specs=inside,
        out_shape=jax.ShapeDtypeStruct((2, rows, pieces[0].shape[2]), BF16),
        compiler_params=params(),
        name="collect",
    )(*pieces, *after)


def partial_kernel(plan, groups, count, waits, *refs):
    raws, (enc_ref, dec_ref), outs, (tokens_ref,) = (
        refs[:count],
        refs[count : count + 2],
        refs[count + 2 + waits : -1],
        refs[-1:],
    )

    @pl.when(pl.program_id(0) == 0)
    def _():
        def store(q, row, values):
            tokens_ref[q, pl.ds(row, 16), :] = values

        place_rows(plan, groups, raws, store)

    rows = outs[0].shape[1]
    for q, weight in enumerate((enc_ref, dec_ref)):
        part = jnp.dot(tokens_ref[q], weight[...], preferred_element_type=F32)
        for i, out in enumerate(outs):
            out[q] = part[i * rows : (i + 1) * rows].astype(out.dtype)


def partials(plan, groups, raws, enc_weight, dec_weight, first, width, after):
    tokens = sum(groups) * plan.rows
    outs = 4 if plan.blocks > 1 else 2
    kinds = (F32, BF16, F32, BF16) if plan.blocks > 1 else (BF16, BF16)
    block = divisor(math.gcd(first, width), 1024)
    base = first // block
    weight = pl.BlockSpec((plan.stack, block), lambda i: (0, base + i))
    inputs = [pl.BlockSpec(raw.shape, lambda i: (0, 0, 0)) for raw in raws]
    out = pl.BlockSpec((2, tokens // outs, block), lambda i: (0, 0, i))
    return pl.pallas_call(
        functools.partial(partial_kernel, plan, groups, len(raws), len(after)),
        grid=(width // block,),
        in_specs=inputs + [weight] * 2 + waiting(after),
        out_specs=[out] * outs,
        out_shape=[jax.ShapeDtypeStruct((2, tokens // outs, width), kind) for kind in kinds],
        scratch_shapes=[pltpu.VMEM((2, tokens, plan.stack), BF16)],
        compiler_params=params(),
        name="partials",
    )(*raws, enc_weight, dec_weight, *after)


def joined_kernel(waits, *refs):
    outs = refs[8 + waits :]
    pieces = len(outs) // 2
    for stream in range(2):
        base = 0
        for kept, got in (refs[4 * stream : 4 * stream + 2], refs[4 * stream + 2 : 4 * stream + 4]):
            total = kept[...].astype(F32) + got[...].astype(F32)
            rows = total.shape[1] // pieces
            for i in range(pieces):
                part = total[:, i * rows : (i + 1) * rows]
                outs[stream * pieces + i][:, base : base + rows] = part.astype(BF16)
            base += rows


def joined(plan, near, far, skip, after):
    pieces = plan.blocks // 2
    width = far[0][0].shape[2]
    block = divisor(math.gcd(skip, width), 1024)
    base = skip // block
    operands, specs = [], []
    for stream in range(2):
        for pair, start in ((near[stream], base), (far[stream], 0)):
            for array in pair:
                operands.append(array)
                specs.append(
                    pl.BlockSpec(
                        (2, array.shape[1], block), lambda i, start=start: (0, 0, start + i)
                    )
                )
    rows = (near[0][0].shape[1] + far[0][0].shape[1]) // pieces
    return pl.pallas_call(
        functools.partial(joined_kernel, len(after)),
        grid=(width // block,),
        in_specs=specs + waiting(after),
        out_specs=[pl.BlockSpec((2, rows, block), lambda i: (0, 0, i))] * (2 * pieces),
        out_shape=[jax.ShapeDtypeStruct((2, rows, width), BF16)] * (2 * pieces),
        compiler_params=params(),
        name="joined",
    )(*operands, *after)


def add_kernel(pieces, waits, *refs):
    outs = refs[4 + waits :]
    for stream in range(2):
        total = refs[2 * stream][...].astype(F32) + refs[2 * stream + 1][...].astype(F32)
        rows = total.shape[1] // pieces
        for i in range(pieces):
            outs[stream * pieces + i][...] = total[:, i * rows : (i + 1) * rows].astype(BF16)


def add(plan, kept, got, pieces, after):
    _, rows, width = kept[0].shape
    block = divisor(width, 1024)
    whole = pl.BlockSpec((2, rows, block), lambda i: (0, 0, i))
    part = pl.BlockSpec((2, rows // pieces, block), lambda i: (0, 0, i))
    return pl.pallas_call(
        functools.partial(add_kernel, pieces, len(after)),
        grid=(width // block,),
        in_specs=[whole] * 4 + waiting(after),
        out_specs=[part] * (2 * pieces),
        out_shape=[jax.ShapeDtypeStruct((2, rows // pieces, width), BF16)] * (2 * pieces),
        compiler_params=params(),
        name="add",
    )(kept[0], got[0], kept[1], got[1], *after)


def gate_kernel(waits, *refs):
    outs = refs[5 + waits :]
    bias = refs[4][...]
    for stream in range(2):
        mine, other = refs[2 * stream], refs[2 * stream + 1]
        scaled = 4.0 * (mine[0].astype(F32) + other[0].astype(F32) + bias)
        code_grad = mine[1].astype(F32) + other[1].astype(F32)
        small = jnp.exp(-jnp.abs(scaled))
        code = 0.25 * (jnp.maximum(scaled, 0.0) + jnp.log1p(small))
        gate = jnp.where(scaled >= 0.0, 1.0, small) / (1.0 + small)
        outs[stream][0] = code.astype(BF16)
        outs[stream][1] = (code_grad * gate).astype(BF16)


def gate(plan, mine, other, bias, first, after):
    _, rows, width = mine[0].shape
    block = divisor(math.gcd(first, width), 1024)
    base = first // block
    whole = pl.BlockSpec((2, rows, block), lambda i: (0, 0, i))
    return pl.pallas_call(
        functools.partial(gate_kernel, len(after)),
        grid=(width // block,),
        in_specs=[whole] * 4 + [pl.BlockSpec((1, block), lambda i: (0, base + i))] + waiting(after),
        out_specs=[whole] * 2,
        out_shape=[jax.ShapeDtypeStruct((2, rows, width), BF16)] * 2,
        compiler_params=params(),
        name="gate",
    )(mine[0], other[0], mine[1], other[1], bias, *after)


def turn_kernel(plan, groups, count, waits, *refs):
    raws, outs, scratch = refs[:count], refs[count + waits : -1], refs[-1]

    def store(q, row, values):
        scratch[q, pl.ds(row, 16), :] = values

    place_rows(plan, groups, raws, store)
    for q in range(2):
        outs[q][...] = scratch[q].T


def turned(plan, groups, raws, after):
    tokens = sum(groups) * plan.rows
    whole = pl.BlockSpec(memory_space=pltpu.VMEM)
    return pl.pallas_call(
        functools.partial(turn_kernel, plan, groups, len(raws), len(after)),
        in_specs=[whole] * len(raws) + waiting(after),
        out_specs=[whole] * 2,
        out_shape=[jax.ShapeDtypeStruct((plan.stack, tokens), BF16)] * 2,
        scratch_shapes=[pltpu.VMEM((2, tokens, plan.stack), BF16)],
        compiler_params=params(),
        name="turned",
    )(*raws, *after)


def grads_kernel(rows, skips, waits, *refs):
    resid_ref, error_ref = refs[:2]
    parts = refs[2 : 2 + len(skips)]
    enc_ref, dec_ref, bias_ref, code_ref, masked_ref = refs[2 + len(skips) + waits :]
    block = code_ref.shape[1]
    here = pl.program_id(0) * block
    left = iter(zip(parts, skips))
    total = None
    for stream in rows:
        blocks = []
        for row in stream:
            part, skip = next(left)
            height = part.shape[1]
            columns = pl.ds(pl.multiple_of(skip + here, 128), block)
            masked = part[1, :, columns]
            code_ref[row : row + height] = part[0, :, columns]
            masked_ref[row : row + height] = masked
            blocks.append(jnp.sum(masked.astype(F32), axis=0, keepdims=True))
        value = tree_sum(blocks)
        total = value if total is None else total + value
    bias_ref[...] = total
    enc_ref[...] = jnp.dot(resid_ref[...], masked_ref[...], preferred_element_type=F32).astype(BF16)
    dec_ref[...] = jnp.dot(error_ref[...], code_ref[...], preferred_element_type=F32).astype(BF16)


def grads(plan, turned_tokens, held, first, width, before, after):
    tokens = turned_tokens[0].shape[1]
    block = divisor(math.gcd(first, width), 1024)
    base = first // block
    parts, skips = [], []
    for arrays, _, origin in held:
        parts += arrays
        skips += [first - origin] * len(arrays)
    inside = pl.BlockSpec(memory_space=pltpu.VMEM)
    extra = list(before) + after
    return pl.pallas_call(
        functools.partial(grads_kernel, [rows for _, rows, _ in held], skips, len(extra)),
        grid=(width // block,),
        in_specs=[inside] * (2 + len(parts)) + waiting(extra),
        out_specs=[
            pl.BlockSpec((plan.stack, block), lambda i: (0, base + i)),
            pl.BlockSpec((plan.stack, block), lambda i: (0, base + i)),
            pl.BlockSpec((1, block), lambda i: (0, base + i)),
        ],
        out_shape=[
            jax.ShapeDtypeStruct((plan.stack, plan.feats), BF16),
            jax.ShapeDtypeStruct((plan.stack, plan.feats), BF16),
            jax.ShapeDtypeStruct((1, plan.feats), F32),
        ],
        scratch_shapes=[pltpu.VMEM((tokens, block), BF16)] * 2,
        input_output_aliases={2 + len(parts) + i: i for i in range(len(before))},
        compiler_params=params(),
        name="grads",
    )(*turned_tokens, *parts, *extra)


class Piece:
    def __init__(self, plan, which, first, width):
        self.plan, self.first, self.width = plan, first, width
        near, far = plan.near, plan.peers - plan.near
        heights = [plan.block_rows(near), plan.block_rows(far)]
        self.groups = {"near": [near], "far": [far], "all": [near, far]}[which]
        base = heights[0] if which == "far" else 0
        self.rows = [
            [(s * plan.blocks + j) * sum(heights) + base for j in range(plan.blocks)]
            for s in range(2)
        ]

    def start(self, raws, enc_weight, dec_weight, early, after):
        plan = self.plan
        self.early = early
        groups = self.groups
        if early is not None:
            groups, raws = groups[1:], raws[plan.near :]
        outs = partials(plan, groups, raws, enc_weight, dec_weight, self.first, self.width, after)
        self.level = 0
        if plan.blocks > 1:
            self.kept = [outs[0], outs[2]]
            self.swap([outs[1], outs[3]])
        else:
            self.kept = list(outs)
            self.swap(self.kept)
        return outs[0]

    def swap(self, sent):
        self.got = [self.plan.swap(sent[s], self.plan.orders[s][self.level]) for s in range(2)]
        self.level += 1

    def add(self, after):
        last = self.plan.bits - 1
        while self.level <= last:
            pieces = 2 if self.level < last else 1
            if self.level == 1 and self.early is not None:
                near = list(zip(self.early.kept, self.early.got))
                far = list(zip(self.kept, self.got))
                cut = joined(self.plan, near, far, self.first - self.early.first, after)
            else:
                cut = add(self.plan, self.kept, self.got, pieces, after)
            after = [cut[0]]
            if pieces == 2:
                self.kept = [cut[0], cut[2]]
                self.swap([cut[1], cut[3]])
            else:
                self.kept = list(cut)
                self.swap(self.kept)
        return after[0]

    def gate(self, bias, after):
        plan = self.plan
        gated = gate(plan, self.kept, self.got, bias, self.first, after)
        self.held = [[gated[0]], [gated[1]]]
        for level in reversed(range(plan.bits - 1)):
            for s in range(2):
                self.held[s] = self.held[s] + [
                    plan.swap(array, plan.orders[s][level]) for array in self.held[s]
                ]
        return gated[0]


PIECES = (("all", 0, 3), ("all", 3, 3), ("all", 6, 3), ("all", 9, 3), ("all", 12, 2), ("all", 14, 2))
GRADS = tuple((first, width) for _, first, width in PIECES)
ORDER = (
    "P0", "P1", "T0", "A0", "A1", "N0", "N1", "P2",
    "G0", "P3", "G1", "A2", "A3", "N2", "N3", "P4",
    "G2", "P5", "G3", "A4", "A5", "N4", "N5", "G4",
    "G5",
)
CHAIN = True
AHEAD = 2


def per_device(plan, residuals, errors, enc_weight, dec_weight, enc_bias):
    feats = plan.feats
    unit = feats // 16
    bias = enc_bias.reshape(1, feats)
    own = jnp.stack([residuals, errors])
    raws = [own] + [plan.peer(own, m) for m in range(1, plan.near)]
    far = [plan.peer(own, m) for m in range(plan.near, plan.peers, 2)]

    pieces = [Piece(plan, which, first * unit, width * unit) for which, first, width in PIECES]
    result, tokens, chain = [], {}, []
    early = None
    if AHEAD and plan.bits > 1 and plan.near < plan.peers:
        ahead = pieces[:AHEAD]
        width = sum(piece.width for piece in ahead)
        early = Piece(plan, "near", ahead[0].first, width)
        chain = [early.start(raws, enc_weight, dec_weight, None, [])]
    if far:
        mine = collect(far, chain)
        raws += [mine, plan.peer(mine, 1)]
    for entry in ORDER:
        op, *behind = entry.split("<")
        step, index = op[0], int(op[1:])
        after = list(chain)
        for name in behind:
            if name[0] == "H":
                after += [part[-1] for part in pieces[int(name[1:])].held]
            else:
                after.append(tokens[name])
        if step == "P":
            covers = early is not None and index < AHEAD
            if covers and index == AHEAD - 1:
                after = after + early.got
            token = pieces[index].start(
                raws, enc_weight, dec_weight, early if covers else None, after
            )
        elif step == "A":
            token = pieces[index].add(after)
        elif step == "N":
            token = pieces[index].gate(bias, after)
        elif step == "T":
            flipped = turned(plan, [plan.near, plan.peers - plan.near], raws, after)
            token = flipped[0]
        else:
            first, width = (unit * v for v in GRADS[index])
            held = []
            for piece in pieces:
                if piece.first <= first < piece.first + piece.width:
                    held += [(piece.held[s], piece.rows[s], piece.first) for s in range(2)]
            result = grads(plan, flipped, held, first, width, result, after)
            token = result[2]
        tokens[op] = token
        chain = [token] if CHAIN else []
    enc_grad, dec_grad, bias_grad = result
    return enc_grad, dec_grad, bias_grad.reshape(feats)


def solution(mesh):
    placed = (
        P("feat", "layer"),
        P("feat", "layer"),
        P("layer", "feat"),
        P("layer", "feat"),
        P("feat"),
    )
    layers, peers = mesh.shape["layer"], mesh.shape["feat"]

    def body(residuals, errors, enc_weight, dec_weight, enc_bias):
        plan = Plan(layers, peers, residuals.shape[0], residuals.shape[1], enc_bias.shape[0])
        return per_device(plan, residuals, errors, enc_weight, dec_weight, enc_bias)

    return jax.shard_map(
        body,
        mesh=mesh,
        in_specs=placed,
        out_specs=(P("layer", "feat"), P("layer", "feat"), P("feat")),
        check_vma=False,
    )
```
